512 devices in a mesh: row: 32 (over z_lo, x, core), col: 16 (over z_hi, y).
Axes of the slice: x: 4, y: 8, z: 8 (z_hi: 2, z_lo: 4; z = z_hi * 4 + z_lo), core: 2. Of those that a mesh axis runs over, the one named last changes fastest.
Arguments:
- pair: bfloat16 [768, 768, 128], P('row', 'col'), may hold values from -6 to 6
- valid: int32 [768], replicated, may hold values 0 or 1
- ln_gain: float32 [128], replicated, may hold values from 0.1 to 1.9
- w_query: bfloat16 [128, 128], replicated, may hold values from -3 to 3
- w_key: bfloat16 [128, 128], replicated, may hold values from -3 to 3
- w_value: bfloat16 [128, 128], replicated, may hold values from -0.5 to 0.5
- w_gate: bfloat16 [128, 128], replicated, may hold values from -0.5 to 0.5
- w_bias: bfloat16 [128, 4], replicated, may hold values from -0.5 to 0.5
- w_out: bfloat16 [128, 128], replicated, may hold values from -0.5 to 0.5
Outputs:
- update: bfloat16 [768, 768, 128], P('row', 'col')
The draws below stay inside these ranges and needn't reach their ends.
All inputs are finite; a program needn't handle non-finite values.
Results may differ from the reference program's by a relative error of at most 0.015.
The reference program's roundings to bfloat16 on the way (of `normed`, `query`, `keys`, `bias` and `gated`) count: a program that leaves them out, or rounds other values in their place, can miss the bound.
Values may be sent and summed in bfloat16 or wider, within the bound.
No kernel may reach another device: no remote copies, remote signals or barrier semaphores. Data moves between devices by JAX's collectives and lax.ppermute only.
A program may use at most 64 MiB of HBM per device.

```python
import jax
import jax.numpy as jnp
from jax import lax

C = 128
HEADS = 4
HEAD_DIM = 32
HD = 128
N = 768


def draw_w_query(key, part):
    key = jax.random.fold_in(key, 11)
    sample = jnp.clip(jax.random.normal(key, (C, HD), jnp.float32), -3.0, 3.0) * 0.09
    return sample.astype(jnp.bfloat16)


def draw_w_key(key, part):
    key = jax.random.fold_in(key, 23)
    sample = jnp.clip(jax.random.normal(key, (C, HD), jnp.float32), -3.0, 3.0) * 0.09
    return sample.astype(jnp.bfloat16)


def with_ends(entries, stream_key, smallest, top_value):
    longest = entries.shape.index(max(entries.shape))
    spots = []
    for shift in (0, 1):
        where = [jax.random.randint(jax.random.fold_in(stream_key, axis), (), 0, length) for axis, length in enumerate(entries.shape)]
        where[longest] = (where[longest] + shift) % entries.shape[longest]
        spots.append(tuple(where))
    return entries.at[spots[0]].set(smallest).at[spots[1]].set(top_value)


def level_of(own_key, extent, shards, least, top_value):
    gain = 1.0
    for position, parts in shards:
        steps = jax.random.uniform(jax.random.fold_in(jax.random.fold_in(own_key, 6), position), (parts,), jnp.float32, least / len(shards), top_value / len(shards))
        gain = gain * jnp.repeat(jnp.exp(steps), extent[position] // parts).reshape((-1,) + (1,) * (len(extent) - 1 - position))
    return gain


def bell_draw(rng, extent, scale, reach, pieces=(), held_as=jnp.bfloat16):
    gain = level_of(rng, extent, pieces, -0.22, 0.18) if pieces else 1.0
    array = jax.random.normal(rng, extent, jnp.float32) * scale * gain
    return jnp.minimum(jnp.maximum(array, -reach), reach).astype(held_as)


def setup_inputs(seed: int = 0) -> dict:
    key_of = jax.random.split(jax.random.key(seed), 10)
    pair = bell_draw(key_of[0], (N, N, C), 1.0, 6.0, ((0, 32), (1, 16)))
    valid = with_ends((jax.random.randint(key_of[1], (N,), 0, 4) < 3).astype(jnp.int32), jax.random.fold_in(key_of[1], 1), 0, 1)
    ln_gain = jnp.clip(1.0 + 0.18 * jax.random.normal(key_of[2], (C,), jnp.float32), 0.1, 1.9)
    w_query = draw_w_query(jax.random.fold_in(key_of[9], 71), 0)
    w_key = draw_w_key(jax.random.fold_in(key_of[9], 71), 0)
    w_value = bell_draw(key_of[5], (C, HD), C ** -0.5, 0.5)
    w_gate = bell_draw(key_of[6], (C, HD), C ** -0.5, 0.5)
    w_bias = bell_draw(key_of[7], (C, HEADS), C ** -0.5, 0.5)
    w_out = bell_draw(key_of[8], (HD, C), HD ** -0.5, 0.5)
    return dict(pair=pair, valid=valid, ln_gain=ln_gain, w_query=w_query, w_key=w_key, w_value=w_value, w_gate=w_gate, w_bias=w_bias, w_out=w_out)


def normalize(pair, ln_gain):
    values = pair.astype(jnp.float32)
    center = lax.optimization_barrier(jnp.mean(values, axis=-1, keepdims=True))
    spread = lax.optimization_barrier(jnp.mean((values - center) ** 2, axis=-1, keepdims=True))
    return ((values - center) * lax.rsqrt(spread + 1e-05) * ln_gain).astype(jnp.bfloat16)

def reference(pair, valid, ln_gain, w_query, w_key, w_value, w_gate, w_bias, w_out):
    normed = normalize(pair, ln_gain)
    flat = normed.reshape(N * N, C)
    query = (jnp.dot(flat, w_query, preferred_element_type=jnp.float32) * HEAD_DIM ** (-0.5)).astype(jnp.bfloat16)
    keys = jnp.dot(flat, w_key, preferred_element_type=jnp.float32).astype(jnp.bfloat16)
    values = jnp.dot(flat, w_value, preferred_element_type=jnp.float32).astype(jnp.bfloat16)
    gate = jax.nn.sigmoid(jnp.dot(flat, w_gate, preferred_element_type=jnp.float32))
    query = query.reshape(N, N, HEADS, HEAD_DIM)
    keys = keys.reshape(N, N, HEADS, HEAD_DIM)
    values = values.reshape(N, N, HEADS, HEAD_DIM)
    gate = gate.reshape(N, N, HD)
    bias = jnp.einsum('jkc,ch->hjk', normed.astype(jnp.float32), w_bias.astype(jnp.float32)).astype(jnp.bfloat16)
    bias_wide = bias.astype(jnp.float32)
    penalty = jnp.where(valid == 1, 0.0, -1000000000.0).astype(jnp.float32)

    def one_row(items):
        row_query, row_keys, row_values, row_gate = items
        scores = jnp.einsum('jhd,khd->hjk', row_query.astype(jnp.float32), row_keys.astype(jnp.float32))
        scores = scores + bias_wide + penalty
        peak = lax.optimization_barrier(jnp.max(scores, axis=-1, keepdims=True))
        weights = jnp.exp(scores - peak)
        total = lax.optimization_barrier(jnp.sum(weights, axis=-1))
        numer = jnp.einsum('hjk,khd->jhd', weights.astype(jnp.bfloat16).astype(jnp.float32), row_values.astype(jnp.float32))
        attended = numer / jnp.transpose(total)[:, :, None]
        return (attended.reshape(N, HD) * row_gate).astype(jnp.bfloat16)
    gated = lax.map(one_row, (query, keys, values, gate))
    update = jnp.dot(gated.reshape(N * N, HD), w_out, preferred_element_type=jnp.float32).astype(jnp.bfloat16)
    return update.reshape(N, N, C)
```

```python
import jax
import jax.numpy as jnp
from jax import lax
from jax.experimental import pallas as pl
from jax.experimental.pallas import tpu as pltpu
from jax.sharding import Mesh
from jax.sharding import PartitionSpec as P

HEADS = 4
HEAD_DIM = 32
ROW = ("zl", "x", "core")
COL = ("zh", "yo", "yi")
NT = (((1,), (1,)), ((), ()))


def head_mask(rows, h):
    lane = lax.broadcasted_iota(jnp.int32, (rows, 128), 1)
    return lane // HEAD_DIM == h


def normalize_kernel(pair_ref, gain_ref, w_ref, normed_ref, bias_ref):
    rows, cols, width = pair_ref.shape
    line = lax.broadcasted_iota(jnp.int32, (128, width), 0)
    w_t = w_ref[...].astype(jnp.float32)
    wide = sum(jnp.where(line // rows == h, w_t[h : h + 1, :], 0.0) for h in range(HEADS))
    acc = jnp.zeros((cols, 128), jnp.float32)
    for j in range(rows):
        values = pair_ref[j].astype(jnp.float32)
        center = jnp.mean(values, axis=-1, keepdims=True)
        shifted = values - center
        spread = jnp.mean(shifted * shifted, axis=-1, keepdims=True)
        normed = (shifted * lax.rsqrt(spread + 1e-05) * gain_ref[...]).astype(jnp.bfloat16)
        normed_ref[j] = normed
        at = jnp.where(line % rows == j, wide, 0.0).astype(jnp.bfloat16)
        acc += lax.dot_general(normed, at, NT, preferred_element_type=jnp.float32)
    bias_ref[...] = acc.astype(jnp.bfloat16)


def normalize(pair, gain, w_bias_t):
    rows, cols, width = pair.shape
    return pl.pallas_call(
        normalize_kernel,
        out_shape=(
            jax.ShapeDtypeStruct((rows, cols, width), jnp.bfloat16),
            jax.ShapeDtypeStruct((cols, 128), jnp.bfloat16),
        ),
        name="normalize",
    )(pair, gain, w_bias_t)


def attend_kernel(
    order_ref, core_ref, *refs
):
    recv_refs, refs = refs[:5], refs[5:]
    own_ref, other_ref, pen_ref, wq_ref, wk_ref, wvt_ref, wg_ref, wo_ref, out_ref, score_bias, folded = refs
    members, rows, cols, width = recv_refs[0].shape
    blocks = sum(ref.shape[0] for ref in recv_refs)
    count = blocks * cols
    here = members * cols
    xs = own_ref.shape[0]
    step = here // (2 * xs)
    lanes = step * HEADS
    first = core_ref[0] == 0

    def lay(k, carry):
        source = pl.ds(pl.multiple_of(order_ref[k] * cols, cols), cols)
        at = pl.ds(pl.multiple_of(k * cols, cols), cols)
        pieces = []
        for x in range(xs):
            own, other = own_ref[x, source, :].astype(jnp.float32), other_ref[x, source, :].astype(jnp.float32)
            pieces.append(jnp.where(first, own, other)[:, :lanes])
            pieces.append(jnp.where(first, other, own)[:, :lanes])
        score_bias[at, :] = jnp.concatenate(pieces, axis=1) + pen_ref[source, :]
        return carry

    lax.fori_loop(0, blocks, lay, 0)

    def one_row(i, carry):
        normed = jnp.concatenate([ref[:, i].reshape(-1, width) for ref in recv_refs], axis=0)
        keys = jnp.dot(normed, wk_ref[...], preferred_element_type=jnp.float32).astype(jnp.bfloat16)
        values_t = lax.dot_general(wvt_ref[...], normed, NT, preferred_element_type=jnp.float32).astype(jnp.bfloat16)
        mine = recv_refs[0][:, i].reshape(here, width)
        query = jnp.dot(mine, wq_ref[...], preferred_element_type=jnp.float32) * HEAD_DIM ** (-0.5)
        query = query.astype(jnp.bfloat16).astype(jnp.float32)
        gate = jax.nn.sigmoid(jnp.dot(mine, wg_ref[...], preferred_element_type=jnp.float32))
        spread = jnp.concatenate(
            [
                jnp.where(head_mask(step, h), query[b * step : (b + 1) * step], 0.0)
                for b in range(here // step)
                for h in range(HEADS)
            ],
            axis=0,
        ).astype(jnp.bfloat16)
        chunk = 256
        for c in range(here * HEADS // chunk):
            at = slice(c * chunk, (c + 1) * chunk)
            scores = lax.dot_general(keys, spread[at], NT, preferred_element_type=jnp.float32) + score_bias[:, at]
            peak = jnp.max(scores, axis=0, keepdims=True)
            weights = jnp.exp(scores - peak)
            total = jnp.sum(weights, axis=0, keepdims=True)
            numer = jnp.dot(values_t, weights.astype(jnp.bfloat16), preferred_element_type=jnp.float32)
            folded[at, :] = (numer / total).T
        attended = jnp.concatenate(
            [
                sum(
                    jnp.where(head_mask(step, h), folded[pl.ds((b * HEADS + h) * step, step), :], 0.0)
                    for h in range(HEADS)
                )
                for b in range(here // step)
            ],
            axis=0,
        )
        gated = (attended * gate).astype(jnp.bfloat16)
        update = jnp.dot(gated, wo_ref[...], preferred_element_type=jnp.float32).astype(jnp.bfloat16)
        out_ref[:, i] = update.reshape(members, cols, width)
        return carry

    lax.fori_loop(0, rows, one_row, 0)


def attend(order, core, recv, own, other, penalty, wq, wk, wvt, wg, wo):
    members, rows, cols, width = recv[0].shape
    here = members * cols
    count = sum(part.shape[0] for part in recv) * cols
    vmem = pl.BlockSpec(memory_space=pltpu.VMEM)
    smem = pl.BlockSpec(memory_space=pltpu.SMEM)
    return pl.pallas_call(
        attend_kernel,
        out_shape=jax.ShapeDtypeStruct((members, rows, cols, width), jnp.bfloat16),
        in_specs=[smem] * 2 + [vmem] * (len(recv) + 8),
        out_specs=vmem,
        scratch_shapes=[
            pltpu.VMEM((count, here * HEADS), jnp.float32),
            pltpu.VMEM((here * HEADS, width), jnp.float32),
        ],
        compiler_params=pltpu.CompilerParams(vmem_limit_bytes=40 * 2**20),
        cost_estimate=pl.CostEstimate(flops=4 * 10**9, bytes_accessed=4 * 10**6, transcendentals=4 * 10**6),
        name="attend",
    )(order, core, *recv, own, other, penalty, wq, wk, wvt, wg, wo)


def gather(block, axes):
    size = lax.axis_size(axes)
    return lax.all_to_all(jnp.broadcast_to(block[None], (size,) + block.shape), axes, 0, 0, tiled=True)


def local(pair, valid, ln_gain, w_query, w_key, w_value, w_gate, w_bias, w_out):
    rows, cols, width = pair.shape
    members = lax.axis_size("yi")
    groups = lax.axis_size(("zh", "yo"))
    core = lax.axis_index("core").astype(jnp.int32).reshape(1)
    group = lax.axis_index(("zh", "yo")).astype(jnp.int32)
    normed, bias = normalize(pair, ln_gain.reshape(1, width), w_bias.T)
    swap = [(a * groups + q, q * groups + a) for a in range(groups) for q in range(groups)]
    bias = lax.ppermute(bias, ("zl", "zh", "yo"), swap)
    flip = [(0, 1), (1, 0)]
    own = lax.all_to_all(normed.reshape(members, rows // members, cols, width), "yi", 0, 0, tiled=True)
    by_z = lax.ppermute(own, "zh", flip)
    by_y = lax.ppermute(own, "yo", flip)
    bias = gather(bias, ("zl", "yi")).reshape(groups * members * cols, 128)
    bias, by_z, by_y = lax.optimization_barrier((bias, by_z, by_y))
    half = members // 2
    far = [lax.ppermute(by_z[:half], "yo", flip), lax.ppermute(by_y[half:], "zh", flip)]
    bias = gather(bias, "x")
    bias, far = lax.optimization_barrier((bias, far))
    other = lax.ppermute(bias, "core", flip)
    penalty = jnp.where(valid == 1, 0.0, -1000000000.0).astype(jnp.float32).reshape(-1, 1)
    order = jnp.concatenate([(group ^ f) * members + jnp.arange(members, dtype=jnp.int32) for f in (0, 2, 1, 3)])
    update = attend(
        order, core, [own, by_z, by_y, *far], bias, other, penalty, w_query, w_key, w_value.T, w_gate, w_out
    )
    update = lax.all_to_all(update, "yi", 0, 0, tiled=True)
    return update.reshape(rows, cols, width)


def solution(mesh):
    fine = Mesh(mesh.devices.reshape(4, 4, 2, 2, 2, 4), ROW + COL)
    return jax.shard_map(
        local,
        mesh=fine,
        in_specs=(P(ROW, COL, None), P(), P(), P(), P(), P(), P(), P(), P()),
        out_specs=P(ROW, COL, None),
        check_vma=False,
    )
```

```python
import functools

import jax
import jax.numpy as jnp
from jax import lax
from jax.experimental import pallas as pl
from jax.experimental.pallas import tpu as pltpu
from jax.sharding import Mesh
from jax.sharding import PartitionSpec as P

HEADS = 4
HEAD_DIM = 32
ROW = ("zl1", "zl0", "x", "core")
COL = ("zh", "y")
NT = (((1,), (1,)), ((), ()))


def head_mask(rows, h):
    lane = lax.broadcasted_iota(jnp.int32, (rows, 128), 1)
    return lane // HEAD_DIM == h


def normalize_kernel(pair_ref, gain_ref, w_ref, sent_ref):
    rows, cols, width = pair_ref.shape
    peers, per = sent_ref.shape[0], sent_ref.shape[1] - 1
    line = lax.broadcasted_iota(jnp.int32, (128, width), 0)
    w_t = w_ref[...].astype(jnp.float32)
    wide = sum(jnp.where(line // rows == h, w_t[h : h + 1, :], 0.0) for h in range(HEADS))
    acc = jnp.zeros((cols, 128), jnp.float32)
    for j in range(rows):
        values = pair_ref[j].astype(jnp.float32)
        center = jnp.mean(values, axis=-1, keepdims=True)
        shifted = values - center
        spread = jnp.mean(shifted * shifted, axis=-1, keepdims=True)
        normed = (shifted * lax.rsqrt(spread + 1e-05) * gain_ref[...]).astype(jnp.bfloat16)
        sent_ref[j // per, j % per] = normed
        at = jnp.where(line % rows == j, wide, 0.0).astype(jnp.bfloat16)
        acc += lax.dot_general(normed, at, NT, preferred_element_type=jnp.float32)
    bias = acc.astype(jnp.bfloat16)
    for peer in range(peers):
        sent_ref[peer, per] = bias


def normalize(pair, gain, w_bias_t, peers):
    rows, cols, width = pair.shape
    return pl.pallas_call(
        normalize_kernel,
        out_shape=jax.ShapeDtypeStruct((peers, rows // peers + 1, cols, width), jnp.bfloat16),
        name="normalize",
    )(pair, gain, w_bias_t)


def project_kernel(own_ref, far_ref, wq_ref, wk_ref, wvt_ref, wg_ref, key_ref, value_ref, query_ref, gate_ref):
    blocks, rows, cols, width = own_ref.shape
    step = cols // 2
    masks = [head_mask(step, h) for h in range(HEADS)]
    for i in range(rows):
        own = own_ref[:, i].reshape(blocks * cols, width)
        normed = jnp.concatenate([own, far_ref[:, i].reshape(blocks * cols, width)], axis=0)
        key_ref[i] = jnp.dot(normed, wk_ref[...], preferred_element_type=jnp.float32).astype(jnp.bfloat16)
        value_ref[i] = lax.dot_general(wvt_ref[...], normed, NT, preferred_element_type=jnp.float32).astype(
            jnp.bfloat16
        )
        query = jnp.dot(own, wq_ref[...], preferred_element_type=jnp.float32) * HEAD_DIM ** (-0.5)
        query = query.astype(jnp.bfloat16).astype(jnp.float32)
        gate = jax.nn.sigmoid(jnp.dot(own, wg_ref[...], preferred_element_type=jnp.float32))
        for half in range(2):
            starts = [b * cols + half * step for b in range(blocks)]
            query_ref[half, i] = jnp.concatenate(
                [jnp.where(masks[h], query[at : at + step], 0.0) for at in starts for h in range(HEADS)], axis=0
            ).astype(jnp.bfloat16)
            gate_ref[half, i] = jnp.concatenate([gate[at : at + step] for at in starts], axis=0)


def project(own, far, wq, wk, wvt, wg):
    blocks, rows, cols, width = own.shape
    count = 2 * blocks * cols
    return pl.pallas_call(
        project_kernel,
        out_shape=(
            jax.ShapeDtypeStruct((rows, count, width), jnp.bfloat16),
            jax.ShapeDtypeStruct((rows, width, count), jnp.bfloat16),
            jax.ShapeDtypeStruct((2, rows, count // 4 * HEADS, width), jnp.bfloat16),
            jax.ShapeDtypeStruct((2, rows, count // 4, width), jnp.float32),
        ),
        compiler_params=pltpu.CompilerParams(vmem_limit_bytes=16 * 2**20),
        cost_estimate=pl.CostEstimate(flops=10**9, bytes_accessed=10**7, transcendentals=10**6),
        name="project",
    )(own, far, wq, wk, wvt, wg)


def attend_kernel(
    first, half_ref, bias_ref, pen_ref, key_ref, value_ref, query_ref, gate_ref, wo_ref, *refs
):
    before_ref, out_ref, score_bias, folded = (None, *refs) if first else refs
    blocks, rows, _, width = out_ref.shape
    count = key_ref.shape[1]
    lanes = query_ref.shape[2] // blocks
    step = lanes // HEADS
    here = blocks * step
    quarter = bias_ref.shape[2]
    part, chunk = 48, 128
    half = half_ref[0]
    masks = [head_mask(step, h) for h in range(HEADS)]

    for k in range(0, count, part):
        z, m, at = k // (HEADS * quarter), k // quarter % HEADS, k % quarter
        pieces = [
            bias_ref[b, z, at : at + part, m * lanes : (m + 1) * lanes].astype(jnp.float32) for b in range(blocks)
        ]
        score_bias[k : k + part, :] = jnp.concatenate(pieces, axis=1) + pen_ref[k : k + part, :]

    for i in range(rows):
        for c in range(0, blocks * lanes, chunk):
            at = slice(c, c + chunk)
            scores = lax.dot_general(key_ref[i], query_ref[half, i, at, :], NT, preferred_element_type=jnp.float32)
            scores = scores + score_bias[:, at]
            peak = jnp.max(scores, axis=0, keepdims=True)
            weights = jnp.exp(scores - peak)
            total = jnp.sum(weights, axis=0, keepdims=True)
            numer = jnp.dot(value_ref[i], weights.astype(jnp.bfloat16), preferred_element_type=jnp.float32)
            folded[i, at, :] = (numer * (1.0 / total)).T

    gated = []
    for i in range(rows):
        attended = [
            sum(
                jnp.where(masks[h], folded[i, (b * HEADS + h) * step : (b * HEADS + h + 1) * step, :], 0.0)
                for h in range(HEADS)
            )
            for b in range(blocks)
        ]
        gated.append((jnp.concatenate(attended, axis=0) * gate_ref[half, i]).astype(jnp.bfloat16))
    update = jnp.dot(jnp.concatenate(gated, axis=0), wo_ref[...], preferred_element_type=jnp.float32)
    for i in range(rows):
        for b in range(blocks):
            mine = update[i * here + b * step : i * here + (b + 1) * step]
            if first:
                out_ref[b, i] = mine
            else:
                other = before_ref[b, i]
                joined = [jnp.where(half == 0, mine, other), jnp.where(half == 0, other, mine)]
                out_ref[b, i] = jnp.concatenate(joined, axis=0).astype(jnp.bfloat16)


def attend(half, bias, penalty, keys, values, query, gate, wo, before=None):
    blocks = bias.shape[0]
    rows, count, width = keys.shape
    here = query.shape[2]
    step = here // HEADS // blocks
    vmem = pl.BlockSpec(memory_space=pltpu.VMEM)
    smem = pl.BlockSpec(memory_space=pltpu.SMEM)
    if before is None:
        out, more = jax.ShapeDtypeStruct((blocks, rows, step, width), jnp.float32), ()
    else:
        out, more = jax.ShapeDtypeStruct((blocks, rows, 2 * step, width), jnp.bfloat16), (before,)
    return pl.pallas_call(
        functools.partial(attend_kernel, before is None),
        out_shape=out,
        in_specs=[smem] + [vmem] * (7 + len(more)),
        out_specs=vmem,
        scratch_shapes=[pltpu.VMEM((count, here), jnp.float32), pltpu.VMEM((rows, here, width), jnp.float32)],
        compiler_params=pltpu.CompilerParams(vmem_limit_bytes=16 * 2**20),
        cost_estimate=pl.CostEstimate(flops=2 * 10**9, bytes_accessed=2 * 10**7, transcendentals=2 * 10**6),
        name="attend",
    )(half, bias, penalty, keys, values, query, gate, wo, *more)


def gather(block, axes):
    size = lax.axis_size(axes)
    return lax.all_to_all(jnp.broadcast_to(block[None], (size,) + block.shape), axes, 0, 0, tiled=True)


def local(pair, valid, ln_gain, w_query, w_key, w_value, w_gate, w_bias, w_out):
    rows, cols, width = pair.shape
    ring = lax.axis_size("y")
    core = lax.axis_index("core").astype(jnp.int32).reshape(1)
    first_z = lax.axis_index("zh") == 0
    flip = [(0, 1), (1, 0)]
    got = lax.all_to_all(normalize(pair, ln_gain.reshape(1, width), w_bias.T, ring), "y", 0, 0, tiled=True)
    bias = got[:, -1].reshape(HEADS, -1, 128)
    bias = jnp.concatenate([bias[m, :, : rows * HEADS] for m in range(HEADS)], axis=1)
    same = lax.ppermute(bias, ("zl1", "zh"), [(0, 0), (1, 2), (2, 1), (3, 3)])
    swap = lax.ppermute(bias, ("zl1", "zh"), [(0, 2), (1, 0), (2, 3), (3, 1)])
    straight = lax.axis_index("zl1") == lax.axis_index("zh")
    bias = jnp.stack([jnp.where(straight, same, swap), jnp.where(straight, swap, same)])
    bias, near = lax.optimization_barrier((bias, got[:, :-1]))
    far = lax.ppermute(near, "zh", flip)
    bias = gather(bias, ("zl0", "x"))
    bias, far = lax.optimization_barrier((bias, far))
    other = lax.ppermute(bias, "core", flip)
    penalty = jnp.where(valid == 1, 0.0, -1000000000.0).astype(jnp.float32).reshape(2, -1)
    penalty = jnp.where(first_z, penalty, penalty[::-1]).reshape(-1, 1)
    parts = project(near, far, w_query, w_key, w_value.T, w_gate)
    update = attend(core, bias, penalty, *parts, w_out)
    update = attend(1 - core, other, penalty, *parts, w_out, update)
    return lax.all_to_all(update, "y", 0, 0, tiled=True).reshape(rows, cols, width)


def solution(mesh):
    fine = Mesh(mesh.devices.reshape(2, 2, 4, 2, 2, 8), ROW + COL)
    return jax.shard_map(
        local,
        mesh=fine,
        in_specs=(P(ROW, COL, None), P(), P(), P(), P(), P(), P(), P(), P()),
        out_specs=P(ROW, COL, None),
        check_vma=False,
    )
```

```python
import functools

import jax
import jax.numpy as jnp
from jax import lax
from jax.experimental import pallas as pl
from jax.experimental.pallas import tpu as pltpu
from jax.sharding import Mesh
from jax.sharding import PartitionSpec as P

HEADS = 4
HEAD_DIM = 32
ROW = ("zl1", "zl0", "x", "core")
COL = ("zh", "y")
NT = (((1,), (1,)), ((), ()))


def head_mask(rows, h):
    lane = lax.broadcasted_iota(jnp.int32, (rows, 128), 1)
    return lane // HEAD_DIM == h


def normalize_kernel(pair_ref, gain_ref, w_ref, sent_ref):
    rows, cols, width = pair_ref.shape
    peers, per = sent_ref.shape[0], sent_ref.shape[1] - 1
    line = lax.broadcasted_iota(jnp.int32, (128, width), 0)
    w_t = w_ref[...].astype(jnp.float32)
    wide = sum(jnp.where(line // rows == h, w_t[h : h + 1, :], 0.0) for h in range(HEADS))
    acc = jnp.zeros((cols, 128), jnp.float32)
    for j in range(rows):
        values = pair_ref[j].astype(jnp.float32)
        center = jnp.mean(values, axis=-1, keepdims=True)
        shifted = values - center
        spread = jnp.mean(shifted * shifted, axis=-1, keepdims=True)
        normed = (shifted * lax.rsqrt(spread + 1e-05) * gain_ref[...]).astype(jnp.bfloat16)
        sent_ref[j // per, j % per] = normed
        at = jnp.where(line % rows == j, wide, 0.0).astype(jnp.bfloat16)
        acc += lax.dot_general(normed, at, NT, preferred_element_type=jnp.float32)
    bias = acc.astype(jnp.bfloat16)
    for peer in range(peers):
        sent_ref[peer, per] = bias


def normalize(pair, gain, w_bias_t, peers):
    rows, cols, width = pair.shape
    return pl.pallas_call(
        normalize_kernel,
        out_shape=jax.ShapeDtypeStruct((peers, rows // peers + 1, cols, width), jnp.bfloat16),
        name="normalize",
    )(pair, gain, w_bias_t)


def project_kernel(own_ref, far_ref, wq_ref, wk_ref, wvt_ref, wg_ref, key_ref, value_ref, query_ref, gate_ref):
    blocks, rows, cols, width = own_ref.shape
    step = cols // 2
    masks = [head_mask(step, h) for h in range(HEADS)]
    for i in range(rows):
        own = own_ref[:, i].reshape(blocks * cols, width)
        normed = jnp.concatenate([own, far_ref[:, i].reshape(blocks * cols, width)], axis=0)
        key_ref[i] = jnp.dot(normed, wk_ref[...], preferred_element_type=jnp.float32).astype(jnp.bfloat16)
        value_ref[i] = lax.dot_general(wvt_ref[...], normed, NT, preferred_element_type=jnp.float32).astype(
            jnp.bfloat16
        )
        query = jnp.dot(own, wq_ref[...], preferred_element_type=jnp.float32) * HEAD_DIM ** (-0.5)
        query = query.astype(jnp.bfloat16).astype(jnp.float32)
        gate = jax.nn.sigmoid(jnp.dot(own, wg_ref[...], preferred_element_type=jnp.float32))
        for half in range(2):
            starts = [b * cols + half * step for b in range(blocks)]
            query_ref[half, i] = jnp.concatenate(
                [jnp.where(masks[h], query[at : at + step], 0.0) for at in starts for h in range(HEADS)], axis=0
            ).astype(jnp.bfloat16)
            gate_ref[half, i] = jnp.concatenate([gate[at : at + step] for at in starts], axis=0)


def project(own, far, wq, wk, wvt, wg):
    blocks, rows, cols, width = own.shape
    count = 2 * blocks * cols
    return pl.pallas_call(
        project_kernel,
        out_shape=(
            jax.ShapeDtypeStruct((rows, count, width), jnp.bfloat16),
            jax.ShapeDtypeStruct((rows, width, count), jnp.bfloat16),
            jax.ShapeDtypeStruct((2, rows, count // 4 * HEADS, width), jnp.bfloat16),
            jax.ShapeDtypeStruct((2, rows, count // 4, width), jnp.float32),
        ),
        compiler_params=pltpu.CompilerParams(vmem_limit_bytes=16 * 2**20),
        cost_estimate=pl.CostEstimate(flops=2 * 10**10, bytes_accessed=10**7, transcendentals=10**6),
        name="project",
    )(own, far, wq, wk, wvt, wg)


def attend_kernel(
    first, half_ref, bias_ref, pen_ref, key_ref, value_ref, query_ref, gate_ref, wo_ref, *refs
):
    before_ref, out_ref, score_bias, folded = (None, *refs) if first else refs
    blocks, rows, _, width = out_ref.shape
    count = key_ref.shape[1]
    lanes = query_ref.shape[2] // blocks
    step = lanes // HEADS
    here = blocks * step
    quarter = bias_ref.shape[2]
    part, chunk = 48, 128
    half = half_ref[0]
    masks = [head_mask(step, h) for h in range(HEADS)]

    for k in range(0, count, part):
        z, m, at = k // (HEADS * quarter), k // quarter % HEADS, k % quarter
        pieces = [
            bias_ref[b, z, at : at + part, m * lanes : (m + 1) * lanes].astype(jnp.float32) for b in range(blocks)
        ]
        score_bias[k : k + part, :] = jnp.concatenate(pieces, axis=1) + pen_ref[k : k + part, :]

    for i in range(rows):
        for c in range(0, blocks * lanes, chunk):
            at = slice(c, c + chunk)
            scores = lax.dot_general(key_ref[i], query_ref[half, i, at, :], NT, preferred_element_type=jnp.float32)
            scores = scores + score_bias[:, at]
            peak = jnp.max(scores, axis=0, keepdims=True)
            weights = jnp.exp(scores - peak)
            total = jnp.sum(weights, axis=0, keepdims=True)
            numer = jnp.dot(value_ref[i], weights.astype(jnp.bfloat16), preferred_element_type=jnp.float32)
            folded[i, at, :] = (numer * (1.0 / total)).T

    gated = []
    for i in range(rows):
        attended = [
            sum(
                jnp.where(masks[h], folded[i, (b * HEADS + h) * step : (b * HEADS + h + 1) * step, :], 0.0)
                for h in range(HEADS)
            )
            for b in range(blocks)
        ]
        gated.append((jnp.concatenate(attended, axis=0) * gate_ref[half, i]).astype(jnp.bfloat16))
    update = jnp.dot(jnp.concatenate(gated, axis=0), wo_ref[...], preferred_element_type=jnp.float32)
    for i in range(rows):
        for b in range(blocks):
            mine = update[i * here + b * step : i * here + (b + 1) * step]
            if first:
                out_ref[b, i] = mine
            else:
                other = before_ref[b, i]
                joined = [jnp.where(half == 0, mine, other), jnp.where(half == 0, other, mine)]
                out_ref[b, i] = jnp.concatenate(joined, axis=0).astype(jnp.bfloat16)


def attend(half, bias, penalty, keys, values, query, gate, wo, before=None):
    blocks = bias.shape[0]
    rows, count, width = keys.shape
    here = query.shape[2]
    step = here // HEADS // blocks
    vmem = pl.BlockSpec(memory_space=pltpu.VMEM)
    smem = pl.BlockSpec(memory_space=pltpu.SMEM)
    if before is None:
        out, more = jax.ShapeDtypeStruct((blocks, rows, step, width), jnp.float32), ()
    else:
        out, more = jax.ShapeDtypeStruct((blocks, rows, 2 * step, width), jnp.bfloat16), (before,)
    return pl.pallas_call(
        functools.partial(attend_kernel, before is None),
        out_shape=out,
        in_specs=[smem] + [vmem] * (7 + len(more)),
        out_specs=vmem,
        scratch_shapes=[pltpu.VMEM((count, here), jnp.float32), pltpu.VMEM((rows, here, width), jnp.float32)],
        compiler_params=pltpu.CompilerParams(vmem_limit_bytes=16 * 2**20),
        cost_estimate=pl.CostEstimate(flops=2 * 10**9, bytes_accessed=2 * 10**7, transcendentals=2 * 10**6),
        name="attend",
    )(half, bias, penalty, keys, values, query, gate, wo, *more)


def gather(block, axes):
    size = lax.axis_size(axes)
    return lax.all_to_all(jnp.broadcast_to(block[None], (size,) + block.shape), axes, 0, 0, tiled=True)


def local(pair, valid, ln_gain, w_query, w_key, w_value, w_gate, w_bias, w_out):
    rows, cols, width = pair.shape
    ring = lax.axis_size("y")
    core = lax.axis_index("core").astype(jnp.int32).reshape(1)
    first_z = lax.axis_index("zh") == 0
    flip = [(0, 1), (1, 0)]
    got = lax.all_to_all(normalize(pair, ln_gain.reshape(1, width), w_bias.T, ring), "y", 0, 0, tiled=True)
    bias = got[:, -1].reshape(HEADS, -1, 128)
    bias = jnp.concatenate([bias[m, :, : rows * HEADS] for m in range(HEADS)], axis=1)
    same = lax.ppermute(bias, ("zl1", "zh"), [(0, 0), (1, 2), (2, 1), (3, 3)])
    swap = lax.ppermute(bias, ("zl1", "zh"), [(0, 2), (1, 0), (2, 3), (3, 1)])
    straight = lax.axis_index("zl1") == lax.axis_index("zh")
    bias = jnp.stack([jnp.where(straight, same, swap), jnp.where(straight, swap, same)])
    bias, near = lax.optimization_barrier((bias, got[:, :-1]))
    far = lax.ppermute(near, "zh", flip)
    bias = gather(bias, ("zl0", "x"))

    other = lax.ppermute(bias, "core", flip)
    penalty = jnp.where(valid == 1, 0.0, -1000000000.0).astype(jnp.float32).reshape(2, -1)
    penalty = jnp.where(first_z, penalty, penalty[::-1]).reshape(-1, 1)
    parts = project(near, far, w_query, w_key, w_value.T, w_gate)
    update = attend(core, bias, penalty, *parts, w_out)
    update = attend(1 - core, other, penalty, *parts, w_out, update)
    return lax.all_to_all(update, "y", 0, 0, tiled=True).reshape(rows, cols, width)


def solution(mesh):
    fine = Mesh(mesh.devices.reshape(2, 2, 4, 2, 2, 8), ROW + COL)
    return jax.shard_map(
        local,
        mesh=fine,
        in_specs=(P(ROW, COL, None), P(), P(), P(), P(), P(), P(), P(), P()),
        out_specs=P(ROW, COL, None),
        check_vma=False,
    )
```

```python
import functools

import jax
import jax.numpy as jnp
from jax import lax
from jax.experimental import pallas as pl
from jax.experimental.pallas import tpu as pltpu
from jax.sharding import Mesh
from jax.sharding import PartitionSpec as P

HEADS = 4
HEAD_DIM = 32
ROW = ("zl1", "zl0", "x", "core")
COL = ("zh", "y")
NT = (((1,), (1,)), ((), ()))


def head_mask(rows, h):
    lane = lax.broadcasted_iota(jnp.int32, (rows, 128), 1)
    return lane // HEAD_DIM == h


def normalize_kernel(pair_ref, gain_ref, w_ref, sent_ref):
    rows, cols, width = pair_ref.shape
    peers, per = sent_ref.shape[0], sent_ref.shape[1] - 1
    line = lax.broadcasted_iota(jnp.int32, (128, width), 0)
    w_t = w_ref[...].astype(jnp.float32)
    wide = sum(jnp.where(line // rows == h, w_t[h : h + 1, :], 0.0) for h in range(HEADS))
    acc = jnp.zeros((cols, 128), jnp.float32)
    for j in range(rows):
        values = pair_ref[j].astype(jnp.float32)
        center = jnp.mean(values, axis=-1, keepdims=True)
        shifted = values - center
        spread = jnp.mean(shifted * shifted, axis=-1, keepdims=True)
        normed = (shifted * lax.rsqrt(spread + 1e-05) * gain_ref[...]).astype(jnp.bfloat16)
        sent_ref[j // per, j % per] = normed
        at = jnp.where(line % rows == j, wide, 0.0).astype(jnp.bfloat16)
        acc += lax.dot_general(normed, at, NT, preferred_element_type=jnp.float32)
    bias = acc.astype(jnp.bfloat16)
    for peer in range(peers):
        sent_ref[peer, per] = bias


def normalize(pair, gain, w_bias_t, peers):
    rows, cols, width = pair.shape
    return pl.pallas_call(
        normalize_kernel,
        out_shape=jax.ShapeDtypeStruct((peers, rows // peers + 1, cols, width), jnp.bfloat16),
        name="normalize",
    )(pair, gain, w_bias_t)


def project_kernel(own_ref, far_ref, wq_ref, wk_ref, wvt_ref, wg_ref, key_ref, value_ref, query_ref, gate_ref):
    blocks, rows, cols, width = own_ref.shape
    step = cols // 2
    masks = [head_mask(step, h) for h in range(HEADS)]
    for i in range(rows):
        own = own_ref[:, i].reshape(blocks * cols, width)
        normed = jnp.concatenate([own, far_ref[:, i].reshape(blocks * cols, width)], axis=0)
        key_ref[i] = jnp.dot(normed, wk_ref[...], preferred_element_type=jnp.float32).astype(jnp.bfloat16)
        value_ref[i] = lax.dot_general(wvt_ref[...], normed, NT, preferred_element_type=jnp.float32).astype(
            jnp.bfloat16
        )
        query = jnp.dot(own, wq_ref[...], preferred_element_type=jnp.float32) * HEAD_DIM ** (-0.5)
        query = query.astype(jnp.bfloat16).astype(jnp.float32)
        gate = jax.nn.sigmoid(jnp.dot(own, wg_ref[...], preferred_element_type=jnp.float32))
        for half in range(2):
            starts = [b * cols + half * step for b in range(blocks)]
            query_ref[half, i] = jnp.concatenate(
                [jnp.where(masks[h], query[at : at + step], 0.0) for at in starts for h in range(HEADS)], axis=0
            ).astype(jnp.bfloat16)
            gate_ref[half, i] = jnp.concatenate([gate[at : at + step] for at in starts], axis=0)


def project(own, far, wq, wk, wvt, wg):
    blocks, rows, cols, width = own.shape
    count = 2 * blocks * cols
    return pl.pallas_call(
        project_kernel,
        out_shape=(
            jax.ShapeDtypeStruct((rows, count, width), jnp.bfloat16),
            jax.ShapeDtypeStruct((rows, width, count), jnp.bfloat16),
            jax.ShapeDtypeStruct((2, rows, count // 4 * HEADS, width), jnp.bfloat16),
            jax.ShapeDtypeStruct((2, rows, count // 4, width), jnp.float32),
        ),
        compiler_params=pltpu.CompilerParams(vmem_limit_bytes=16 * 2**20),
        cost_estimate=pl.CostEstimate(flops=2 * 10**10, bytes_accessed=10**7, transcendentals=10**6),
        name="project",
    )(own, far, wq, wk, wvt, wg)


def attend_kernel(
    first, half_ref, bias_ref, pen_ref, key_ref, value_ref, query_ref, gate_ref, wo_ref, *refs
):
    before_ref, out_ref, score_bias, folded = (None, *refs) if first else refs
    blocks, rows, _, width = out_ref.shape
    count = key_ref.shape[1]
    lanes = query_ref.shape[2] // blocks
    step = lanes // HEADS
    here = blocks * step
    xs, quarter = bias_ref.shape[0], bias_ref.shape[3]
    part, chunk = 48, 128
    half = half_ref[0]
    masks = [head_mask(step, h) for h in range(HEADS)]

    for k in range(0, count, part):
        z, m, at = k // (HEADS * quarter), k // quarter % HEADS, k % quarter
        pieces = [
            bias_ref[b % xs, b // xs, z, at : at + part, m * lanes : (m + 1) * lanes].astype(jnp.float32)
            for b in range(blocks)
        ]
        score_bias[k : k + part, :] = jnp.concatenate(pieces, axis=1) + pen_ref[k : k + part, :]

    for i in range(rows):
        for c in range(0, blocks * lanes, chunk):
            at = slice(c, c + chunk)
            scores = lax.dot_general(key_ref[i], query_ref[half, i, at, :], NT, preferred_element_type=jnp.float32)
            scores = scores + score_bias[:, at]
            peak = jnp.max(scores, axis=0, keepdims=True)
            weights = jnp.exp(scores - peak)
            total = jnp.sum(weights, axis=0, keepdims=True)
            numer = jnp.dot(value_ref[i], weights.astype(jnp.bfloat16), preferred_element_type=jnp.float32)
            folded[i, at, :] = (numer * (1.0 / total)).T

    gated = []
    for i in range(rows):
        attended = [
            sum(
                jnp.where(masks[h], folded[i, (b * HEADS + h) * step : (b * HEADS + h + 1) * step, :], 0.0)
                for h in range(HEADS)
            )
            for b in range(blocks)
        ]
        gated.append((jnp.concatenate(attended, axis=0) * gate_ref[half, i]).astype(jnp.bfloat16))
    update = jnp.dot(jnp.concatenate(gated, axis=0), wo_ref[...], preferred_element_type=jnp.float32)
    for i in range(rows):
        for b in range(blocks):
            mine = update[i * here + b * step : i * here + (b + 1) * step]
            if first:
                out_ref[b, i] = mine
            else:
                other = before_ref[b, i]
                joined = [jnp.where(half == 0, mine, other), jnp.where(half == 0, other, mine)]
                out_ref[b, i] = jnp.concatenate(joined, axis=0).astype(jnp.bfloat16)


def attend(half, bias, penalty, keys, values, query, gate, wo, before=None):
    blocks = bias.shape[0] * bias.shape[1]
    rows, count, width = keys.shape
    here = query.shape[2]
    step = here // HEADS // blocks
    vmem = pl.BlockSpec(memory_space=pltpu.VMEM)
    smem = pl.BlockSpec(memory_space=pltpu.SMEM)
    if before is None:
        out, more = jax.ShapeDtypeStruct((blocks, rows, step, width), jnp.float32), ()
    else:
        out, more = jax.ShapeDtypeStruct((blocks, rows, 2 * step, width), jnp.bfloat16), (before,)
    return pl.pallas_call(
        functools.partial(attend_kernel, before is None),
        out_shape=out,
        in_specs=[smem] + [vmem] * (7 + len(more)),
        out_specs=vmem,
        scratch_shapes=[pltpu.VMEM((count, here), jnp.float32), pltpu.VMEM((rows, here, width), jnp.float32)],
        compiler_params=pltpu.CompilerParams(vmem_limit_bytes=16 * 2**20),
        cost_estimate=pl.CostEstimate(flops=2 * 10**9, bytes_accessed=2 * 10**7, transcendentals=2 * 10**6),
        name="attend",
    )(half, bias, penalty, keys, values, query, gate, wo, *more)


def gather(block, axes):
    size = lax.axis_size(axes)
    return lax.all_to_all(jnp.broadcast_to(block[None], (size,) + block.shape), axes, 0, 0, tiled=True)


def local(pair, valid, ln_gain, w_query, w_key, w_value, w_gate, w_bias, w_out):
    rows, cols, width = pair.shape
    ring = lax.axis_size("y")
    core = lax.axis_index("core").astype(jnp.int32).reshape(1)
    first_z = lax.axis_index("zh") == 0
    flip = [(0, 1), (1, 0)]
    got = lax.all_to_all(normalize(pair, ln_gain.reshape(1, width), w_bias.T, ring), "y", 0, 0, tiled=True)
    bias = got[:, -1].reshape(HEADS, -1, 128)
    bias = jnp.concatenate([bias[m, :, : rows * HEADS] for m in range(HEADS)], axis=1)
    low = lax.axis_index("zl0") == 0
    straight = lax.axis_index("zl1") == lax.axis_index("zh")
    beside = lax.ppermute(bias, "zl0", flip)
    bias = jnp.stack([jnp.where(low, bias, beside), jnp.where(low, beside, bias)])
    same = lax.ppermute(bias, ("zl1", "zh"), [(0, 0), (1, 2), (2, 1), (3, 3)])
    swap = lax.ppermute(bias, ("zl1", "zh"), [(0, 2), (1, 0), (2, 3), (3, 1)])
    bias = jnp.stack([jnp.where(straight, same, swap), jnp.where(straight, swap, same)], axis=1)
    bias, near = lax.optimization_barrier((bias, got[:, :-1]))
    far = lax.ppermute(near, "zh", flip)
    bias = gather(bias, "x")
    other = lax.ppermute(bias, "core", flip)
    penalty = jnp.where(valid == 1, 0.0, -1000000000.0).astype(jnp.float32).reshape(2, -1)
    penalty = jnp.where(first_z, penalty, penalty[::-1]).reshape(-1, 1)
    parts = project(near, far, w_query, w_key, w_value.T, w_gate)
    update = attend(core, bias, penalty, *parts, w_out)
    update = attend(1 - core, other, penalty, *parts, w_out, update)
    return lax.all_to_all(update, "y", 0, 0, tiled=True).reshape(rows, cols, width)


def solution(mesh):
    fine = Mesh(mesh.devices.reshape(2, 2, 4, 2, 2, 8), ROW + COL)
    return jax.shard_map(
        local,
        mesh=fine,
        in_specs=(P(ROW, COL, None), P(), P(), P(), P(), P(), P(), P(), P()),
        out_specs=P(ROW, COL, None),
        check_vma=False,
    )
```

```python
import functools

import jax
import jax.numpy as jnp
from jax import lax
from jax.experimental import pallas as pl
from jax.experimental.pallas import tpu as pltpu
from jax.sharding import Mesh
from jax.sharding import PartitionSpec as P

HEADS = 4
HEAD_DIM = 32
ROW = ("zl1", "zl0", "x", "core")
COL = ("zh", "y")
NT = (((1,), (1,)), ((), ()))


def head_mask(rows, h):
    lane = lax.broadcasted_iota(jnp.int32, (rows, 128), 1)
    return lane // HEAD_DIM == h


def normalize_kernel(pair_ref, gain_ref, w_ref, sent_ref):
    rows, cols, width = pair_ref.shape
    peers, per = sent_ref.shape[0], sent_ref.shape[1] - 1
    line = lax.broadcasted_iota(jnp.int32, (128, width), 0)
    w_t = w_ref[...].astype(jnp.float32)
    wide = sum(jnp.where(line // rows == h, w_t[h : h + 1, :], 0.0) for h in range(HEADS))
    acc = jnp.zeros((cols, 128), jnp.float32)
    for j in range(rows):
        values = pair_ref[j].astype(jnp.float32)
        center = jnp.mean(values, axis=-1, keepdims=True)
        shifted = values - center
        spread = jnp.mean(shifted * shifted, axis=-1, keepdims=True)
        normed = (shifted * lax.rsqrt(spread + 1e-05) * gain_ref[...]).astype(jnp.bfloat16)
        sent_ref[j // per, j % per] = normed
        at = jnp.where(line % rows == j, wide, 0.0).astype(jnp.bfloat16)
        acc += lax.dot_general(normed, at, NT, preferred_element_type=jnp.float32)
    bias = acc.astype(jnp.bfloat16)
    for peer in range(peers):
        sent_ref[peer, per] = bias


def normalize(pair, gain, w_bias_t, peers):
    rows, cols, width = pair.shape
    return pl.pallas_call(
        normalize_kernel,
        out_shape=jax.ShapeDtypeStruct((peers, rows // peers + 1, cols, width), jnp.bfloat16),
        name="normalize",
    )(pair, gain, w_bias_t)


def project_kernel(own_ref, far_ref, wq_ref, wk_ref, wvt_ref, wg_ref, key_ref, value_ref, query_ref, gate_ref):
    blocks, rows, cols, width = own_ref.shape
    step = cols // 2
    masks = [head_mask(step, h) for h in range(HEADS)]
    for i in range(rows):
        own = own_ref[:, i].reshape(blocks * cols, width)
        normed = jnp.concatenate([own, far_ref[:, i].reshape(blocks * cols, width)], axis=0)
        key_ref[i] = jnp.dot(normed, wk_ref[...], preferred_element_type=jnp.float32).astype(jnp.bfloat16)
        value_ref[i] = lax.dot_general(wvt_ref[...], normed, NT, preferred_element_type=jnp.float32).astype(
            jnp.bfloat16
        )
        query = jnp.dot(own, wq_ref[...], preferred_element_type=jnp.float32) * HEAD_DIM ** (-0.5)
        query = query.astype(jnp.bfloat16).astype(jnp.float32)
        gate = jax.nn.sigmoid(jnp.dot(own, wg_ref[...], preferred_element_type=jnp.float32))
        for half in range(2):
            starts = [b * cols + half * step for b in range(blocks)]
            query_ref[half, i] = jnp.concatenate(
                [jnp.where(masks[h], query[at : at + step], 0.0) for at in starts for h in range(HEADS)], axis=0
            ).astype(jnp.bfloat16)
            gate_ref[half, i] = jnp.concatenate([gate[at : at + step] for at in starts], axis=0)


def project(own, far, wq, wk, wvt, wg):
    blocks, rows, cols, width = own.shape
    count = 2 * blocks * cols
    return pl.pallas_call(
        project_kernel,
        out_shape=(
            jax.ShapeDtypeStruct((rows, count, width), jnp.bfloat16),
            jax.ShapeDtypeStruct((rows, width, count), jnp.bfloat16),
            jax.ShapeDtypeStruct((2, rows, count // 4 * HEADS, width), jnp.bfloat16),
            jax.ShapeDtypeStruct((2, rows, count // 4, width), jnp.float32),
        ),
        compiler_params=pltpu.CompilerParams(vmem_limit_bytes=16 * 2**20),
        cost_estimate=pl.CostEstimate(flops=2 * 10**10, bytes_accessed=10**7, transcendentals=10**6),
        name="project",
    )(own, far, wq, wk, wvt, wg)


def attend_kernel(
    first, half_ref, bias_ref, pen_ref, key_ref, value_ref, query_ref, gate_ref, wo_ref, *refs
):
    before_ref, out_ref, score_bias, folded = (None, *refs) if first else refs
    blocks, rows, _, width = out_ref.shape
    count = key_ref.shape[1]
    lanes = query_ref.shape[2] // blocks
    step = lanes // HEADS
    here = blocks * step
    xs, quarter = bias_ref.shape[0], bias_ref.shape[3]
    part, chunk = 48, 128
    half = half_ref[0]
    masks = [head_mask(step, h) for h in range(HEADS)]

    for k in range(0, count, part):
        z, m, at = k // (HEADS * quarter), k // quarter % HEADS, k % quarter
        pieces = [
            bias_ref[b % xs, b // xs, z, at : at + part, m * lanes : (m + 1) * lanes].astype(jnp.float32)
            for b in range(blocks)
        ]
        score_bias[k : k + part, :] = jnp.concatenate(pieces, axis=1) + pen_ref[k : k + part, :]

    for i in range(rows):
        for c in range(0, blocks * lanes, chunk):
            at = slice(c, c + chunk)
            scores = lax.dot_general(key_ref[i], query_ref[half, i, at, :], NT, preferred_element_type=jnp.float32)
            scores = scores + score_bias[:, at]
            peak = jnp.max(scores, axis=0, keepdims=True)
            weights = jnp.exp(scores - peak)
            total = jnp.sum(weights, axis=0, keepdims=True)
            numer = jnp.dot(value_ref[i], weights.astype(jnp.bfloat16), preferred_element_type=jnp.float32)
            folded[i, at, :] = (numer * (1.0 / total)).T

    gated = []
    for i in range(rows):
        attended = [
            sum(
                jnp.where(masks[h], folded[i, (b * HEADS + h) * step : (b * HEADS + h + 1) * step, :], 0.0)
                for h in range(HEADS)
            )
            for b in range(blocks)
        ]
        gated.append((jnp.concatenate(attended, axis=0) * gate_ref[half, i]).astype(jnp.bfloat16))
    update = jnp.dot(jnp.concatenate(gated, axis=0), wo_ref[...], preferred_element_type=jnp.float32)
    for i in range(rows):
        for b in range(blocks):
            mine = update[i * here + b * step : i * here + (b + 1) * step]
            if first:
                out_ref[b, i] = mine
            else:
                other = before_ref[b, i]
                joined = [jnp.where(half == 0, mine, other), jnp.where(half == 0, other, mine)]
                out_ref[b, i] = jnp.concatenate(joined, axis=0).astype(jnp.bfloat16)


def attend(half, bias, penalty, keys, values, query, gate, wo, before=None):
    blocks = bias.shape[0] * bias.shape[1]
    rows, count, width = keys.shape
    here = query.shape[2]
    step = here // HEADS // blocks
    vmem = pl.BlockSpec(memory_space=pltpu.VMEM)
    smem = pl.BlockSpec(memory_space=pltpu.SMEM)
    if before is None:
        out, more = jax.ShapeDtypeStruct((blocks, rows, step, width), jnp.float32), ()
    else:
        out, more = jax.ShapeDtypeStruct((blocks, rows, 2 * step, width), jnp.bfloat16), (before,)
    return pl.pallas_call(
        functools.partial(attend_kernel, before is None),
        out_shape=out,
        in_specs=[smem] + [vmem] * (7 + len(more)),
        out_specs=vmem,
        scratch_shapes=[pltpu.VMEM((count, here), jnp.float32), pltpu.VMEM((rows, here, width), jnp.float32)],
        compiler_params=pltpu.CompilerParams(vmem_limit_bytes=16 * 2**20),
        cost_estimate=pl.CostEstimate(flops=2 * 10**9, bytes_accessed=2 * 10**7, transcendentals=2 * 10**6),
        name="attend",
    )(half, bias, penalty, keys, values, query, gate, wo, *more)


def gather(block, axes):
    size = lax.axis_size(axes)
    return lax.all_to_all(jnp.broadcast_to(block[None], (size,) + block.shape), axes, 0, 0, tiled=True)


def local(pair, valid, ln_gain, w_query, w_key, w_value, w_gate, w_bias, w_out):
    rows, cols, width = pair.shape
    ring = lax.axis_size("y")
    core = lax.axis_index("core").astype(jnp.int32).reshape(1)
    first_z = lax.axis_index("zh") == 0
    flip = [(0, 1), (1, 0)]
    got = lax.all_to_all(normalize(pair, ln_gain.reshape(1, width), w_bias.T, ring), "y", 0, 0, tiled=True)
    bias = got[:, -1].reshape(HEADS, -1, 128)
    bias = jnp.concatenate([bias[m, :, : rows * HEADS] for m in range(HEADS)], axis=1)
    low = lax.axis_index("zl0") == 0
    straight = lax.axis_index("zl1") == lax.axis_index("zh")
    beside = lax.ppermute(bias, "zl0", flip)
    bias = jnp.stack([jnp.where(low, bias, beside), jnp.where(low, beside, bias)])
    same = lax.ppermute(bias, ("zl1", "zh"), [(0, 0), (1, 2), (2, 1), (3, 3)])
    swap = lax.ppermute(bias, ("zl1", "zh"), [(0, 2), (1, 0), (2, 3), (3, 1)])
    bias = jnp.stack([jnp.where(straight, same, swap), jnp.where(straight, swap, same)], axis=1)
    near = got[:, :-1]
    far = lax.ppermute(near, "zh", flip)
    bias = gather(bias, "x")
    other = lax.ppermute(bias, "core", flip)
    penalty = jnp.where(valid == 1, 0.0, -1000000000.0).astype(jnp.float32).reshape(2, -1)
    penalty = jnp.where(first_z, penalty, penalty[::-1]).reshape(-1, 1)
    parts = project(near, far, w_query, w_key, w_value.T, w_gate)
    update = attend(core, bias, penalty, *parts, w_out)
    update = attend(1 - core, other, penalty, *parts, w_out, update)
    return lax.all_to_all(update, "y", 0, 0, tiled=True).reshape(rows, cols, width)


def solution(mesh):
    fine = Mesh(mesh.devices.reshape(2, 2, 4, 2, 2, 8), ROW + COL)
    return jax.shard_map(
        local,
        mesh=fine,
        in_specs=(P(ROW, COL, None), P(), P(), P(), P(), P(), P(), P(), P()),
        out_specs=P(ROW, COL, None),
        check_vma=False,
    )
```
